128 devices in a mesh: dp: 16 (over x, y_hi, core), tensor: 8 (over y_lo, z).
Axes of the slice: x: 4, y: 4 (y_hi: 2, y_lo: 2; y = y_hi * 2 + y_lo), z: 4, core: 2. Of those that a mesh axis runs over, the one named last changes fastest.
Arguments:
- tokens: bfloat16 [20480, 1024], P(('dp', 'tensor')), may hold values from -6 to 6
- kept: int32 [64], P('dp'), may hold values from 0 to 256
- w_qkv: bfloat16 [2, 1024, 3, 1024], P(None, 'dp', None, 'tensor'), may hold values from -0.1875 to 0.1875
- w_out: bfloat16 [2, 1024, 1024], P(None, 'tensor', 'dp'), may hold values from -1.75 to 1.75
- w_up: bfloat16 [2, 1024, 4096], P(None, 'dp', 'tensor'), may hold values from -0.1875 to 0.1875
- w_down: bfloat16 [2, 4096, 1024], P(None, 'tensor', 'dp'), may hold values from -0.09375 to 0.09375
- ln_gains: float32 [2, 2, 1024], P(None, None, ('dp', 'tensor')), may hold values from 0.5 to 1.5
- biases: float32 [2, 10, 1024], P(None, None, ('dp', 'tensor')), may hold values from -3 to 3
- grad_out: float32 [20480, 1024], P(('dp', 'tensor')), may hold values from -6 to 6
Outputs:
- activations: float32 [20480, 1024], P(('dp', 'tensor'))
- input_grad: float32 [20480, 1024], P(('dp', 'tensor'))
- qkv_grad: float32 [2, 1024, 3, 1024], P(None, 'dp', None, 'tensor')
- proj_grad: float32 [2, 1024, 1024], P(None, 'tensor', 'dp')
- up_grad: float32 [2, 1024, 4096], P(None, 'dp', 'tensor')
- down_grad: float32 [2, 4096, 1024], P(None, 'tensor', 'dp')
- gain_grad: float32 [2, 2, 1024], P(None, None, ('dp', 'tensor'))
- bias_grad: float32 [2, 10, 1024], P(None, None, ('dp', 'tensor'))
The draws below stay inside these ranges and needn't reach their ends.
All inputs are finite; a program needn't handle non-finite values.
Results may differ from the reference program's by a relative error of at most 0.022.
Values may be sent and summed in bfloat16 or wider, within the bound.
No kernel may reach another device: no remote copies, remote signals or barrier semaphores. Data moves between devices by JAX's collectives and lax.ppermute only.
A program may use at most 192 MiB of HBM per device.

```python
import math
import jax
import jax.numpy as jnp
from jax import lax

D = 1024
HEADS = 16
HEAD = 64
FF = 4096
SEQ = 320
BUFFER = 64
LAYERS = 2
IMG_DEV = 4
IMAGES = 64
TOKENS = 20480


def set_ends(values, stream_key, smallest, high):
    longest = values.shape.index(max(values.shape))
    spots = []
    for shift in (0, 1):
        where = [jax.random.randint(jax.random.fold_in(stream_key, axis), (), 0, length) for axis, length in enumerate(values.shape)]
        where[longest] = (where[longest] + shift) % values.shape[longest]
        spots.append(tuple(where))
    return values.at[spots[0]].set(smallest).at[spots[1]].set(high)


def block_scale(stream_key, shape, cuts, low, high):
    loudness = 1.0
    for axis_at, shards_of in cuts:
        steps = jax.random.uniform(jax.random.fold_in(jax.random.fold_in(stream_key, 6), axis_at), (shards_of,), jnp.float32, low / len(cuts), high / len(cuts))
        loudness = loudness * jnp.repeat(jnp.exp(steps), shape[axis_at] // shards_of).reshape((-1,) + (1,) * (len(shape) - 1 - axis_at))
    return loudness


def gaussian(key, shape, deviation, limit, cuts=(), kind=jnp.bfloat16):
    level = block_scale(key, shape, cuts, -0.22, 0.18) if cuts else 1.0
    array = jax.random.normal(key, shape, jnp.float32) * deviation * level
    return jnp.minimum(jnp.maximum(array, -limit), limit).astype(kind)


def setup_inputs(seed: int = 0) -> dict:
    key_of = jax.random.split(jax.random.key(seed), 10)
    return {
        "tokens": gaussian(key_of[0], (TOKENS, D), 1.0, 6.0, ((0, 128),)),
        "kept": set_ends(jax.random.randint(key_of[1], (IMAGES,), 0, SEQ - BUFFER + 1), jax.random.fold_in(key_of[1], 1), 0, SEQ - BUFFER).astype(jnp.int32),
        "w_qkv": gaussian(key_of[2], (LAYERS, D, 3, D), D ** -0.5, 0.1875, ((1, 16), (3, 8))),
        "w_out": gaussian(key_of[3], (LAYERS, D, D), (4 * D // SEQ) ** -0.5, 1.75, ((1, 8), (2, 16))),
        "w_up": gaussian(key_of[4], (LAYERS, D, FF), D ** -0.5, 0.1875, ((1, 16), (2, 8))),
        "w_down": gaussian(key_of[5], (LAYERS, FF, D), FF ** -0.5, 0.09375, ((1, 8), (2, 16))),
        "ln_gains": jnp.clip(1.0 + 0.1 * jax.random.normal(key_of[6], (LAYERS, 2, D), jnp.float32), 0.5, 1.5),
        "biases": gaussian(key_of[7], (LAYERS, 10, D), 0.5, 3.0, ((2, 128),), jnp.float32),
        "grad_out": gaussian(key_of[8], (TOKENS, D), 1.0, 6.0, ((0, 128),), jnp.float32),
    }


EPS = 1e-06
NEG = -1e+30

@jax.custom_vjp
def low(v):
    return lax.optimization_barrier(v.astype(jnp.bfloat16)).astype(jnp.float32)

@jax.custom_vjp
def low_back(v):
    return v

def low_keep(v):
    return (low(v), None)

def low_pass(kept, grad):
    return (grad,)

def back_keep(v):
    return (v, None)

def back_low(kept, grad):
    return (low(grad),)
low.defvjp(low_keep, low_pass)
low_back.defvjp(back_keep, back_low)

def layer_norm(rows, gain, shift):
    centre = rows - lax.optimization_barrier(jnp.mean(rows, axis=-1, keepdims=True))
    spread = lax.optimization_barrier(jnp.mean(centre * centre, axis=-1, keepdims=True))
    return centre * lax.rsqrt(spread + EPS) * gain + shift

def reference(tokens, kept, w_qkv, w_out, w_up, w_down, ln_gains, biases, grad_out):
    highest = lax.Precision.HIGHEST
    factor = 1.0 / math.sqrt(HEAD)
    groups = IMAGES // IMG_DEV
    position = jnp.arange(SEQ, dtype=jnp.int32)
    valid = position[None, :] < (BUFFER + kept.astype(jnp.int32))[:, None]
    valid_blocks = valid.reshape(groups, IMG_DEV, SEQ)

    def attend(block):
        query, keys, values, allowed = block
        scores = low_back(jnp.einsum('ishd,ithd->ihst', query, keys, precision=highest) * factor)
        scores = jnp.where(allowed[:, None, None, :], scores, NEG)
        top = lax.optimization_barrier(jnp.max(scores, axis=-1, keepdims=True))
        expo = jnp.exp(scores - top)
        probs = expo / lax.optimization_barrier(jnp.sum(expo, axis=-1, keepdims=True))
        return jnp.einsum('ihst,ithd->ishd', low(probs), values, precision=highest)

    def layer(rows, wq, wo, wu, wd, gain, shift):
        normed = low(layer_norm(rows, gain[0], shift[0]))
        stacked = jnp.einsum('td,dce->tce', normed, wq, precision=highest)
        query = low_back(low(stacked[:, 0] + shift[4]))
        keys = low_back(low(stacked[:, 1]))
        values = low_back(low(stacked[:, 2] + shift[5]))
        shape = (groups, IMG_DEV, SEQ, HEADS, HEAD)
        mixed = lax.map(jax.checkpoint(attend), (query.reshape(shape), keys.reshape(shape), values.reshape(shape), valid_blocks))
        mixed = low_back(low(mixed.reshape(TOKENS, D)))
        rows = rows + low_back(jnp.dot(mixed, wo, precision=highest)) + shift[2]
        second = low(layer_norm(rows, gain[1], shift[1]))
        hidden = low_back(jnp.dot(second, wu, precision=highest) + shift[6:10].reshape(FF))
        active = low(jax.nn.gelu(hidden, approximate=False))
        return rows + low_back(jnp.dot(active, wd, precision=highest)) + shift[3]

    def forward(start, wq, wo, wu, wd, gains, shifts):
        rows = start
        for index in range(LAYERS):
            rows = layer(rows, wq[index], wo[index], wu[index], wd[index], gains[index], shifts[index])
        return rows
    inputs = (tokens.astype(jnp.float32), w_qkv.astype(jnp.float32), w_out.astype(jnp.float32), w_up.astype(jnp.float32), w_down.astype(jnp.float32), ln_gains, biases)
    result, pull = jax.vjp(forward, *inputs)
    grads = pull(grad_out)
    return (result, grads[0], grads[1], grads[2], grads[3], grads[4], grads[5], grads[6])
```

```python
import functools
import math

import jax
import jax.numpy as jnp
from jax import lax
from jax.experimental import pallas as pl
from jax.experimental.pallas import tpu as pltpu
from jax.sharding import PartitionSpec as P

HEAD = 64
BUFFER = 64
EPS = 1e-06
NEG = -1e30
BF = jnp.bfloat16
F32 = jnp.float32
LANES = 128
ROWS = 12
FLOPS_PER_US = 1.15e9

PLACES = ("dp", "tensor")
DEVICES = 128
X_MASKS = (32, 64, 96)
YH, CORE, YL, ZH, ZL = 16, 8, 4, 2, 1
Y_MASKS = (YL, YH, YH | YL)
Z_MASK = ZH | ZL

ANY = pl.BlockSpec(memory_space=pl.ANY)
HBM = pl.BlockSpec(memory_space=pltpu.HBM)
VMEM = pl.BlockSpec(memory_space=pltpu.VMEM)
SMEM = pl.BlockSpec(memory_space=pltpu.SMEM)
WINDOW = pl.BlockSpec()


def swapped(array, mask):
    return lax.ppermute(array, PLACES, [(i, i ^ mask) for i in range(DEVICES)])


def sent_by(array, mask, sends):
    return lax.ppermute(array, PLACES, [(i, i ^ mask) for i in range(DEVICES) if sends(i)])


def zl_is_core(place):
    return place & ZL == (place & CORE) // CORE


def zl_is_not_core(place):
    return not zl_is_core(place)


def dot(left, right):
    return jnp.dot(left, right, preferred_element_type=F32)


def dot_turned(left, right):
    return lax.dot_general(left, right, (((1,), (1,)), ((), ())), preferred_element_type=F32)


def outer(left, right):
    return lax.dot_general(left, right, (((0,), (0,)), ((), ())), preferred_element_type=F32)


def call(body, outs, in_specs, args, scratch=(), out_specs=None, limit=12, deps=(), cost=0.5):
    out_specs = tuple(out_specs or [VMEM] * len(outs))
    outs = [
        pltpu.HBM(o.shape, o.dtype) if spec is WINDOW else o
        for o, spec in zip(outs, out_specs)
    ]
    args = [
        pltpu.with_memory_space_constraint(a, pltpu.HBM) if spec is WINDOW else a
        for a, spec in zip(args, in_specs)
    ]
    inputs = len(args)

    def kernel(*refs):
        body(*refs[:inputs], *refs[inputs + len(deps) :])

    windowed = any(spec.block_shape is not None for spec in in_specs)
    return pl.pallas_call(
        kernel,
        grid=(1,) if windowed else (),
        out_shape=tuple(outs),
        in_specs=[*in_specs, *[ANY] * len(deps)],
        out_specs=out_specs,
        scratch_shapes=list(scratch),
        compiler_params=pltpu.CompilerParams(vmem_limit_bytes=limit << 20),
        cost_estimate=pl.CostEstimate(
            flops=int(cost * FLOPS_PER_US), bytes_accessed=1, transcendentals=0
        ),
    )(*args, *deps)


def shape(dims, dtype):
    return jax.ShapeDtypeStruct(tuple(dims), dtype)


def bundle_scratch(wide):
    return pltpu.VMEM((4, 2, LANES, 2 * wide), BF)


def line_piece(lines, last, first):
    if last == 2:
        return lines[2 + first // 2].at[first % 2]
    return lines[(0, 1, None, 4)[last]].at[first]


def bundle_copies(core, wide, lines, whole, sems, inward):
    made = []
    for last in range(4):
        for first in range(4):
            x = last + core * (first - last)
            y = first + core * (last - first)
            at = pl.multiple_of((y % 2) * wide, LANES)
            ends = (line_piece(lines, last, first), whole.at[x, y // 2, :, pl.ds(at, wide)])
            made.append(
                pltpu.make_async_copy(*(ends if inward else ends[::-1]), sems.at[4 * last + first])
            )
    return made


def along(array, number, last):
    masks = (X_MASKS, Y_MASKS) if last else (Y_MASKS, X_MASKS)
    pairs = [
        (i, i ^ masks[1 if i & CORE else 0][number - 1]) for i in range(DEVICES)
    ]
    return lax.ppermute(array, PLACES, pairs)


def shard_kernel(w_qkv, w_out, w_up, w_down, out):
    wide, hidden = w_qkv.shape[3], w_up.shape[2]
    for layer in range(2):
        at = 4 * wide * layer
        for k in range(3):
            out[:, at + k * wide : at + (k + 1) * wide] = w_qkv[layer, k]
        out[:, at + 3 * wide : at + 4 * wide] = w_out[layer]
        at = 8 * wide + 2 * hidden * layer
        out[:, at : at + hidden] = w_up[layer]
        out[:, at + hidden : at + 2 * hidden] = w_down[layer]


def both_kernel(scal, mine, other, out):
    rows = mine.shape[0]
    out[pl.ds(pl.multiple_of(scal[2] * rows, rows), rows), :] = mine[...]
    out[pl.ds(pl.multiple_of((1 - scal[2]) * rows, rows), rows), :] = other[...]


def begin_kernel(layer, scal, both, by_zl, by_zh, by_both, out):
    mine = scal[1] != 0
    attn = by_zh.shape[1] // 2
    feed = by_zl.shape[1] - attn
    cols = slice(attn * layer, attn * (layer + 1))
    rest = slice(2 * attn + feed * layer, 2 * attn + feed * (layer + 1))
    out[:, :attn] = jnp.where(mine, both[:, cols], by_zl[:, :attn])
    out[:, attn : 2 * attn] = jnp.where(mine, by_zh[:, cols], by_both[:, cols])
    out[:, 2 * attn :] = jnp.where(mine, both[:, rest], by_zl[:, attn:])


def cores_joined(shard, scal, deps):
    return call(
        both_kernel,
        [shape((2 * shard.shape[0], shard.shape[1]), BF)],
        [SMEM, VMEM, VMEM],
        [scal, shard, swapped(shard, CORE)],
        deps=deps,
    )[0]


def begun(both, scal, attn, deps=()):
    feed = both.shape[1] // 2 - attn
    part = both[:, : 2 * attn]
    far = [sent_by(part, m, zl_is_core) for m in (ZH, Z_MASK)]
    outs = []
    for layer in range(2):
        first = 2 * attn + feed * layer
        cols = (both[:, attn * layer : attn * (layer + 1)], both[:, first : first + feed])
        near = sent_by(jnp.concatenate(cols, axis=1), ZL, zl_is_core)
        outs.append(
            call(
                functools.partial(begin_kernel, layer),
                [shape((both.shape[0], 2 * attn + feed), BF)],
                [SMEM] + [VMEM] * 4,
                [scal, both, near, *far],
                deps=() if layer else deps,
            )[0]
        )
    return outs


def block(array, axis, at, parts):
    dims = tuple(n // parts if k == axis else n for k, n in enumerate(array.shape))
    place = tuple(at if k == axis else 0 for k in range(array.ndim))
    return pl.BlockSpec(dims, lambda *_: place), dims


def copies_kernel(*refs):
    half = len(refs) // 2
    for source, out in zip(refs[:half], refs[half:]):
        out[...] = source[...]


def halves_of(near, far, deps=(), axis=0):
    specs = [block(near, axis, 0, 2), block(far, axis, 1, 2)]
    return call(
        copies_kernel,
        [shape(dims, BF) for _, dims in specs],
        [spec for spec, _ in specs],
        [near, far],
        deps=deps,
    )


def line_kernel(*refs):
    for k in range(4):
        refs[4][k] = refs[k][...]


class Light:
    def __init__(self, begin, deps=()):
        self.begin = begin
        self.near, self.far = along(begin, 1, False), along(begin, 3, False)
        self.halves = halves_of(self.near, self.far, deps, 1)
        one, two = self.halves
        self.across = [along(one, 3, False), along(two, 1, False)]

    def line(self, k, deps=()):
        specs = [block(a, 1, k, 2) for a in (self.begin, self.near, self.far)]
        across = self.across[k]
        specs.insert(2, (VMEM, across.shape))
        return call(
            line_kernel,
            [shape((4, *across.shape), BF)],
            [spec for spec, _ in specs],
            [self.begin, self.near, across, self.far],
            deps=deps,
        )[0]


def tie_kernel(*refs):
    refs[-1][...] = refs[0][...]


def tied(array, deps):
    return call(tie_kernel, [shape(array.shape, array.dtype)], [VMEM], [array], deps=deps)[0]


class Heavy:
    def __init__(self, line, deps=()):
        self.line = line
        self.near, self.far = along(line, 1, True), along(line, 3, True)
        self.halves = halves_of(self.near, self.far, deps)
        one, two = self.halves
        self.across = [along(one, 3, True), along(two, 1, True)]

    def lines(self):
        return [self.line, self.near, *self.across, self.far]


def sum_kernel(count, *refs):
    total = refs[0][...].astype(F32)
    for ref in refs[1:count]:
        total = total + ref[...].astype(F32)
    total = total.astype(BF)
    outs = refs[count:]
    if len(outs) == 1:
        outs[0][...] = total
        return
    if len(outs) == 4:
        for k, out in enumerate(outs):
            out[...] = total[k]
        return
    keep, send = outs
    for k in range(2):
        keep[k] = total[k]
        send[k] = total[3 - k]


def halves_kernel(keep, moved, mine, send):
    total = (keep[...].astype(F32) + moved[...].astype(F32)).astype(BF)
    mine[...] = total[0]
    send[...] = total[1]


def summed(arrays, outs, deps=()):
    return call(
        functools.partial(sum_kernel, len(arrays)),
        outs,
        [VMEM] * len(arrays),
        arrays,
        deps=deps,
    )


def pass_on_kernel(near, far, to_far, to_near, near_out, far_out):
    half = near.shape[0] // 2
    near_out[:half] = near[:half]
    near_out[half:] = (near[half:].astype(F32) + to_near[...].astype(F32)).astype(BF)
    far_out[:half] = (far[:half].astype(F32) + to_far[...].astype(F32)).astype(BF)
    far_out[half:] = far[half:]


class Reduction:
    def __init__(self, lines):
        self.lines = lines

    def a(self, deps=()):
        mine, near, across_one, across_two, far = self.lines
        moved = [along(across_one, 1, True), along(across_two, 3, True)]
        self.passed = call(
            pass_on_kernel,
            [shape(near.shape, BF)] * 2,
            [VMEM] * 4,
            [near, far, *moved],
            deps=deps,
        )
        return self.passed[:1]

    def b(self, deps=(), direct=False):
        near, far = self.passed
        mine = self.lines[0]
        outs = [shape((2, *mine.shape[1:]), BF)] * 2
        if direct:
            outs = [shape(mine.shape[1:], BF)] * 4
        self.parts = summed([mine, along(near, 1, True), along(far, 3, True)], outs, deps)
        return self.parts[:1]

    def c(self, deps=()):
        keep, send = self.parts
        outs = [shape(keep.shape[1:], BF)] * 2
        self.pair = call(
            halves_kernel, outs, [VMEM] * 2, [keep, along(send, 3, False)], deps=deps
        )
        return self.pair[:1]

    def spread(self):
        return [along(self.parts[k], k, False) for k in (1, 2, 3)]

    def direct(self, moved, deps=()):
        outs = [shape(moved[0].shape, BF)]
        self.total = summed([self.parts[0], *moved], outs, deps)[0]

    def d(self, deps=()):
        mine, send = self.pair
        outs = [shape(mine.shape, BF)]
        self.total = summed([mine, along(send, 1, False)], outs, deps)[0]
        return [self.total]


class Bundle:
    def __init__(self, lines, blocks, places):
        self.lines = lines
        self.blocks = blocks
        self.wide = lines[0].shape[2]
        self.step = 2 * self.wide // blocks
        self.places = places

    def scratch(self):
        return [bundle_scratch(self.wide), pltpu.SemaphoreType.DMA((16,))]

    def out_shapes(self):
        return [shape(l.shape, BF) for l in self.lines]

    def copies(self, core, refs, scratch, inward):
        return bundle_copies(core, self.wide, refs, scratch[0], scratch[1], inward)

    def columns(self, scratch, name, blocks=None):
        first, wide = self.places[name]
        blocks = tuple(range(self.blocks)) if blocks is None else blocks
        cuts = [
            scratch[0][:, :, :, b * self.step + first : b * self.step + first + wide]
            for b in blocks
        ]
        whole = jnp.concatenate(cuts, axis=-1) if len(cuts) > 1 else cuts[0]
        return whole.reshape(-1, wide * len(blocks))

    def store(self, scratch, name, value, x):
        first, wide = self.places[name]
        value = value.reshape(2, LANES, -1)
        for b in range(self.blocks):
            scratch[0][x, :, :, b * self.step + first : b * self.step + first + wide] = value[
                :, :, b * wide : (b + 1) * wide
            ]


def start(copies):
    for copy in copies:
        copy.start()


def finish(copies):
    for copy in copies:
        copy.wait()


def both_rows(own, other):
    return jnp.concatenate([own[...], other[...]])


def lane_halves(value):
    lane = lax.broadcasted_iota(jnp.int32, value.shape, 1)
    zero = jnp.zeros_like(value)
    return jnp.where(lane < HEAD, value, zero), jnp.where(lane < HEAD, zero, value)


def attention_kernel(weights, layer, scal, own, other, small, *refs):
    pieces, refs = refs[:5], refs[5:]
    mine, theirs, qkv, probs, mixed = refs[:5]
    scratch = refs[5:]
    core, valid = scal[2], scal[3]
    copies = weights.copies(core, pieces, scratch, True)
    start(copies)
    rows = own.shape[0]
    seq = 2 * rows
    a = both_rows(own, other)
    finish(copies)
    wide = qkv.shape[1] // 3
    places = [
        pl.multiple_of(
            (((scal[4] ^ ylr) * 4 + (scal[5] ^ zhr) * 2 + core) ^ scal[0]) * LANES, LANES
        )
        for ylr in range(2)
        for zhr in range(2)
    ]
    for k, name in enumerate("qkv"):
        part = dot(a, weights.columns(scratch, name))
        if name != "k":
            at = layer * ROWS + (6 if name == "q" else 7)
            bias = [small[at : at + 1, pl.ds(place, LANES)] for place in places]
            part = part + jnp.concatenate(bias, axis=1)
        qkv[:, k * wide : (k + 1) * wide] = part.astype(BF)
    key = lax.broadcasted_iota(jnp.int32, (1, seq), 1)
    position = jnp.where(key < rows, key + core * rows, key - core * rows)
    allowed = position < valid
    factor = 1.0 / math.sqrt(HEAD)
    for b in range(wide // LANES):
        lanes = slice(b * LANES, (b + 1) * LANES)
        q = qkv[:, b * LANES : (b + 1) * LANES]
        k = qkv[:, wide + b * LANES : wide + (b + 1) * LANES]
        v = qkv[:, 2 * wide + b * LANES : 2 * wide + (b + 1) * LANES]
        total = None
        for h, (q_h, v_h) in enumerate(zip(lane_halves(q), lane_halves(v))):
            scores = jnp.where(allowed, dot_turned(q_h, k) * factor, NEG)
            expo = jnp.exp(scores - jnp.max(scores, axis=-1, keepdims=True))
            p = (expo / jnp.sum(expo, axis=-1, keepdims=True)).astype(BF)
            probs[2 * b + h] = p
            part = dot(p, v_h)
            total = part if total is None else total + part
        mixed[:, lanes] = total.astype(BF)
    out = dot_turned(mixed[...], weights.columns(scratch, "o"))
    mine[...] = out[:rows]
    theirs[...] = out[rows:].astype(BF)


def attention(weights, layer, scal, own, other, small, deps):
    rows, width = own.shape
    wide = width // 2
    seq = 2 * rows
    outs = [
        shape((rows, width), F32),
        shape((rows, width), BF),
        shape((seq, 3 * wide), BF),
        shape((wide // HEAD, seq, seq), BF),
        shape((seq, wide), BF),
    ]
    return call(
        functools.partial(attention_kernel, weights, layer),
        outs,
        [SMEM, VMEM, VMEM, VMEM] + [HBM] * 5,
        [scal, own, other, small, *weights.lines],
        weights.scratch(),
        out_specs=[VMEM, VMEM, WINDOW, WINDOW, WINDOW],
        deps=deps,
        cost=6.0,
    )


def attention_back_kernel(weights, scal, own, other, qkv, probs, *refs):
    pieces, refs = refs[:5], refs[5:]
    mine, theirs, grads = refs[:3]
    scratch = refs[3:]
    copies = weights.copies(scal[2], pieces, scratch, True)
    start(copies)
    rows = own.shape[0]
    wide = qkv.shape[1] // 3
    d = both_rows(own, other)
    finish(copies)
    factor = 1.0 / math.sqrt(HEAD)
    spread = dot(d, weights.columns(scratch, "o")).astype(BF)
    for b in range(wide // LANES):
        q = qkv[:, b * LANES : (b + 1) * LANES]
        k = qkv[:, wide + b * LANES : wide + (b + 1) * LANES]
        v = qkv[:, 2 * wide + b * LANES : 2 * wide + (b + 1) * LANES]
        do = spread[:, b * LANES : (b + 1) * LANES]
        dq = dk = dv = None
        parts = zip(lane_halves(q), lane_halves(k), lane_halves(do))
        for h, (q_h, k_h, do_h) in enumerate(parts):
            p = probs[2 * b + h]
            dv_h = outer(p, do_h)
            dp = dot_turned(do_h, v)
            wide_p = p.astype(F32)
            ds = wide_p * (dp - jnp.sum(wide_p * dp, axis=-1, keepdims=True))
            ds = ds.astype(BF)
            dq_h = dot(ds, k_h)
            dk_h = outer(ds, q_h)
            dq, dk, dv = (
                (dq_h, dk_h, dv_h) if dq is None else (dq + dq_h, dk + dk_h, dv + dv_h)
            )
        grads[:, b * LANES : (b + 1) * LANES] = (dq * factor).astype(BF)
        grads[:, wide + b * LANES : wide + (b + 1) * LANES] = (dk * factor).astype(BF)
        grads[:, 2 * wide + b * LANES : 2 * wide + (b + 1) * LANES] = dv.astype(BF)
    whole = jnp.concatenate([weights.columns(scratch, name) for name in "qkv"], axis=1)
    out = dot_turned(grads[...], whole)
    mine[...] = out[:rows]
    theirs[...] = out[rows:].astype(BF)


def attention_back(weights, scal, own, other, qkv, probs, deps=()):
    rows, width = own.shape
    seq, wide = qkv.shape[0], qkv.shape[1] // 3
    outs = [shape((rows, width), F32), shape((rows, width), BF), shape(qkv.shape, BF)]
    return call(
        functools.partial(attention_back_kernel, weights),
        outs,
        [SMEM, VMEM, VMEM, WINDOW, WINDOW] + [HBM] * 5,
        [scal, own, other, qkv, probs, *weights.lines],
        weights.scratch(),
        deps=deps,
        cost=7.0,
    )


def weight_grad_kernel(weights, jobs, lefts, rights, sums, scal, *refs):
    values = []
    for count in (*lefts, *rights):
        values.append(jnp.concatenate([r[...] for r in refs[:count]]) if count > 1 else refs[0])
        refs = refs[count:]
    pieces, refs = refs[:5], refs[5:]
    sum_refs, scratch = refs[: len(sums)], refs[len(sums) :]
    for name, left, right, first, wide in jobs:
        block = values[left].shape[1] // 4
        for x in range(4):
            grad = outer(
                values[left][:, x * block : (x + 1) * block],
                values[len(lefts) + right][:, first : first + wide],
            )
            weights.store(scratch, name, grad.astype(BF), x)
    copies = weights.copies(scal[2], pieces, scratch, False)
    start(copies)
    for ref, k in zip(sum_refs, sums):
        ref[...] = jnp.sum(values[len(lefts) + k][...].astype(F32), axis=0, keepdims=True)
    finish(copies)


def weight_grads(weights, scal, jobs, lefts, rights, kept, sums, deps=()):
    outs = weights.out_shapes() + [shape((1, rights[k][0].shape[1]), F32) for k in sums]
    arrays = [a for group in (*lefts, *rights) for a in group]
    rows = sum(a.shape[0] for a in lefts[0])
    return call(
        functools.partial(
            weight_grad_kernel,
            weights,
            jobs,
            [len(g) for g in lefts],
            [len(g) for g in rights],
            sums,
        ),
        outs,
        [SMEM]
        + [VMEM] * sum(len(g) for g in lefts)
        + [WINDOW if k in kept else VMEM for k, g in enumerate(rights) for _ in g],
        [scal, *arrays],
        weights.scratch(),
        out_specs=[HBM] * 5 + [VMEM] * len(sums),
        deps=deps,
        cost=5.0,
    )


def hidden_places(scal, layer, ylr):
    row = (scal[4] ^ ylr) * 2 + scal[5]
    mask = lax.broadcasted_iota(jnp.int32, (4, LANES), 0) == row
    return mask, [pl.multiple_of(((scal[2] * 4 + k) ^ scal[0]) * LANES, LANES) for k in range(4)]


def feed_kernel(weights, layer, scal, own, other, small, *refs):
    pieces, refs = refs[:5], refs[5:]
    mine, theirs, active, slope = refs[:4]
    scratch = refs[4:]
    copies = weights.copies(scal[2], pieces, scratch, True)
    start(copies)
    rows = own.shape[0]
    b = both_rows(own, other)
    finish(copies)
    wide = active.shape[1] // 2
    for k in range(2):
        cols = slice(k * wide, (k + 1) * wide)
        mask, places = hidden_places(scal, layer, k)
        at = layer * ROWS + 8
        bias = [jnp.where(mask, small[at : at + 4, pl.ds(p, LANES)], 0.0) for p in places]
        bias = jnp.sum(jnp.concatenate(bias, axis=1), axis=0, keepdims=True)
        u = dot(b, weights.columns(scratch, "u", (k,))) + bias
        below = 0.5 + 0.5 * lax.erf(u * math.sqrt(0.5))
        active[:, cols] = (u * below).astype(BF)
        bell = jnp.exp(u * u * -0.5) * (1.0 / math.sqrt(2.0 * math.pi))
        slope[:, cols] = (below + u * bell).astype(BF)
    out = dot_turned(active[...], weights.columns(scratch, "d"))
    mine[...] = out[:rows]
    theirs[...] = out[rows:].astype(BF)


def feed(weights, layer, scal, own, other, small, deps=()):
    rows, width = own.shape
    seq, wide = 2 * rows, width
    outs = [
        shape((rows, width), F32),
        shape((rows, width), BF),
        shape((seq, wide), BF),
        shape((seq, wide), BF),
    ]
    return call(
        functools.partial(feed_kernel, weights, layer),
        outs,
        [SMEM, VMEM, VMEM, VMEM] + [HBM] * 5,
        [scal, own, other, small, *weights.lines],
        weights.scratch(),
        out_specs=[VMEM, VMEM, WINDOW, WINDOW],
        deps=deps,
        cost=3.5,
    )


def feed_back_kernel(weights, scal, own, other, slope, *refs):
    pieces, refs = refs[:5], refs[5:]
    mine, theirs, grads = refs[:3]
    scratch = refs[3:]
    copies = weights.copies(scal[2], pieces, scratch, True)
    start(copies)
    rows = own.shape[0]
    g = both_rows(own, other)
    finish(copies)
    wide = slope.shape[1] // 2
    for k in range(2):
        cols = slice(k * wide, (k + 1) * wide)
        dz = dot(g, weights.columns(scratch, "d", (k,)))
        grads[:, cols] = (dz * slope[:, cols].astype(F32)).astype(BF)
    out = dot_turned(grads[...], weights.columns(scratch, "u"))
    mine[...] = out[:rows]
    theirs[...] = out[rows:].astype(BF)


def feed_back(weights, scal, own, other, slope, deps=()):
    rows, width = own.shape
    outs = [shape((rows, width), F32), shape((rows, width), BF), shape(slope.shape, BF)]
    return call(
        functools.partial(feed_back_kernel, weights),
        outs,
        [SMEM, VMEM, VMEM, WINDOW] + [HBM] * 5,
        [scal, own, other, slope, *weights.lines],
        weights.scratch(),
        deps=deps,
        cost=3.3,
    )


def in_order(ref, order):
    wide = ref.shape[1] // 8
    return jnp.concatenate(
        [ref[:, pl.ds(pl.multiple_of((k ^ order) * wide, wide), wide)] for k in range(8)], axis=1
    )


def normed(rows, gain, shift):
    centre = rows - jnp.mean(rows, axis=-1, keepdims=True)
    spread = jnp.mean(centre * centre, axis=-1, keepdims=True)
    return centre * lax.rsqrt(spread + EPS) * gain + shift


def first_kernel(scal, mine, moved, small, state, out):
    stays = scal[1] != 0
    order = scal[0]
    rows = jnp.where(stays, in_order(mine, order).astype(F32), in_order(moved, order).astype(F32))
    state[...] = rows
    out[...] = normed(rows, small[0:1], small[2:3]).astype(BF)


def first_rows(scal, mine, moved, small):
    outs = [shape(mine.shape, F32), shape(mine.shape, BF)]
    return call(
        first_kernel,
        outs,
        [SMEM] + [VMEM] * 3,
        [scal, mine, moved, small],
        out_specs=[WINDOW, VMEM],
    )


def grad_kernel(scal, mine, moved, state, out, sums):
    stays = scal[1] != 0
    order = scal[0]
    rows = jnp.where(stays, in_order(mine, order), in_order(moved, order))
    state[...] = rows
    out[...] = rows.astype(BF)
    sums[...] = jnp.sum(rows, axis=0, keepdims=True)


def grad_rows(scal, mine, moved):
    outs = [shape(mine.shape, F32), shape(mine.shape, BF), shape((1, mine.shape[1]), F32)]
    return call(grad_kernel, outs, [SMEM] + [VMEM] * 2, [scal, mine, moved])


def last_kernel(scal, mine, moved, out):
    stays = scal[1] != 0
    order = scal[0]
    out[...] = jnp.where(stays, in_order(mine, order), in_order(moved, order))


def last_rows(scal, mine):
    moved = sent_by(mine, CORE | ZL, zl_is_not_core)
    return call(
        last_kernel, [shape(mine.shape, F32)], [SMEM] + [VMEM] * 2, [scal, mine, moved]
    )[0]


def total_of(refs):
    total = refs[0][...].astype(F32)
    for ref in refs[1:]:
        total = total + ref[...].astype(F32)
    return total


def join_kernel(at, rows, small, *refs):
    *parts, state, out = refs
    bias, gain, shift = (small[k : k + 1] for k in at)
    total = rows[...] + (total_of(parts) + bias)
    state[...] = total
    out[...] = normed(total, gain, shift).astype(BF)


def joined(rows, parts, small, at, deps=()):
    outs = [shape(rows.shape, F32), shape(rows.shape, BF)]
    return call(
        functools.partial(join_kernel, at),
        outs,
        [WINDOW, VMEM] + [VMEM] * len(parts),
        [rows, small, *parts],
        out_specs=[WINDOW, VMEM],
        deps=deps,
        cost=2.0,
    )


def norm_back_kernel(at, above, rows, small, *refs):
    *parts, state, out, sums = refs
    dy = total_of(parts)
    centre = rows[...] - jnp.mean(rows[...], axis=-1, keepdims=True)
    scale = lax.rsqrt(jnp.mean(centre * centre, axis=-1, keepdims=True) + EPS)
    unit = centre * scale
    weighed = dy * small[at : at + 1]
    inner = weighed - jnp.mean(weighed, axis=-1, keepdims=True)
    inner = inner - unit * jnp.mean(weighed * unit, axis=-1, keepdims=True)
    total = above[...] + inner * scale
    state[...] = total
    out[...] = total.astype(BF)
    sums[0:1] = jnp.sum(dy * unit, axis=0, keepdims=True)
    sums[1:2] = jnp.sum(dy, axis=0, keepdims=True)
    sums[2:3] = jnp.sum(total, axis=0, keepdims=True)


def norm_back(above, rows, parts, small, at, deps=()):
    outs = [shape(rows.shape, F32), shape(rows.shape, BF), shape((3, rows.shape[1]), F32)]
    return call(
        functools.partial(norm_back_kernel, at),
        outs,
        [VMEM, WINDOW, VMEM] + [VMEM] * len(parts),
        [above, rows, small, *parts],
        deps=deps,
        cost=1.7,
    )


def fold_kernel(mine, theirs, out):
    out[...] = (mine[...] + theirs[...].astype(F32)).astype(BF)


def folded(mine, theirs):
    return call(
        fold_kernel, [shape(mine.shape, BF)], [VMEM] * 2, [mine, swapped(theirs, CORE)]
    )[0]


def from_far(mine, theirs):
    return swapped(folded(mine, theirs), Z_MASK)


def gathered_rows(own):
    far = swapped(own, Z_MASK)
    return own, swapped(own, CORE), far, swapped(far, CORE)


def gathered_small(small, lane):
    part = jnp.zeros((small.shape[0], LANES), F32)
    part = lax.dynamic_update_slice(part, small, (0, lane))
    steps = [part + swapped(part, YL)]
    for mask in (YH | YL, X_MASKS[0]):
        steps.append(jnp.concatenate([steps[-1], swapped(steps[-1], mask)], axis=1))
    half = steps[-1].shape[1] // 2
    moved = swapped(steps[-1], X_MASKS[2])
    steps.append(jnp.concatenate([steps[-1], moved[:, half:], moved[:, :half]], axis=1))
    for mask in (CORE, Z_MASK, ZL):
        steps.append(steps[-1] + swapped(steps[-1], mask))
    return steps


def summed_over(small, masks):
    for mask in masks:
        small = small + swapped(small, mask)
    return small


def reduced_small(small, lane, wide):
    steps = []
    half = small.shape[1] // 2
    quarter = half // 2
    send = jnp.concatenate([small[:, half + quarter :], small[:, half : half + quarter]], axis=1)
    steps.append(small[:, :half] + swapped(send, X_MASKS[2]))
    for mask in (X_MASKS[0], YH | YL):
        half = steps[-1].shape[1] // 2
        steps.append(steps[-1][:, :half] + swapped(steps[-1][:, half:], mask))
    small = summed_over(steps[-1], [YL])
    return steps, lax.dynamic_slice(small, (0, lane), (small.shape[0], wide))


def pack_kernel(layers, scal, *refs):
    out = refs[-1]
    out[...] = jnp.zeros(out.shape, F32)
    for layer in range(layers):
        one, two, above, heads, hidden = refs[5 * layer : 5 * layer + 5]
        at = layer * ROWS
        out[at : at + 1] = one[0:1]
        out[at + 1 : at + 2] = two[0:1]
        out[at + 2 : at + 3] = one[1:2]
        out[at + 3 : at + 4] = two[1:2]
        out[at + 4 : at + 5] = two[2:3]
        out[at + 5 : at + 6] = above[above.shape[0] - 1 : above.shape[0]]
        wide = heads.shape[1] // 3
        for k in range(4):
            block = (scal[4] ^ (k // 2)) * 4 + (scal[5] ^ (k % 2)) * 2 + scal[2]
            place = pl.multiple_of((block ^ scal[0]) * LANES, LANES)
            for row, first in ((6, 0), (7, 2 * wide)):
                first += k * LANES
                out[at + row : at + row + 1, pl.ds(place, LANES)] = heads[:, first : first + LANES]
        for ylr in range(2):
            mask, places = hidden_places(scal, layer, ylr)
            for k, place in enumerate(places):
                first = (4 * ylr + k) * LANES
                part = jnp.where(mask, hidden[:, first : first + LANES], 0.0)
                out[at + 8 : at + 12, pl.ds(place, LANES)] += part


def packed(scal, parts):
    arrays = [a for layer in parts for a in layer]
    out = shape((ROWS * len(parts), arrays[0].shape[1]), F32)
    return call(
        functools.partial(pack_kernel, len(parts)), [out], [SMEM] + [VMEM] * len(arrays), [scal, *arrays]
    )[0]


def per_device(tokens, kept, w_qkv, w_out, w_up, w_down, ln_gains, biases, grad_out):
    dp_place = lax.axis_index("dp")
    tensor_place = lax.axis_index("tensor")
    core = dp_place % 2
    order = dp_place // 2
    yl = tensor_place // 4
    zh = (tensor_place // 2) % 2
    zl = tensor_place % 2
    rows, width = tokens.shape
    layers = w_qkv.shape[0]
    head_wide = w_qkv.shape[3]
    hidden_wide = w_up.shape[2]

    both_kept = jnp.where(zl == core, kept, swapped(kept, CORE))
    valid = BUFFER + lax.dynamic_index_in_dim(both_kept, yl * 2 + zh, keepdims=False)
    scal = jnp.stack(
        [order, (zl == core).astype(jnp.int32), core, valid.astype(jnp.int32), yl, zh, zl]
    ).astype(jnp.int32)
    own_wide = ln_gains.shape[2]
    lane = (core * 8 + tensor_place) * own_wide

    h, f = head_wide, hidden_wide

    row_weights = [
        w_qkv.transpose(0, 2, 1, 3),
        w_out.transpose(0, 2, 1),
        w_up,
        w_down.transpose(0, 2, 1),
    ]

    shard = call(
        shard_kernel,
        [shape((w_up.shape[1], 8 * h + 4 * f), BF)],
        [WINDOW] * 4,
        row_weights,
    )[0]
    small = jnp.concatenate([ln_gains, biases], axis=1).reshape(layers * ROWS, own_wide)
    steps = gathered_small(tied(small, [shard]), lane)
    small = steps[-1]

    both = cores_joined(shard, scal, ())
    begin, later = begun(both, scal, 4 * h, [steps[2]])
    light = Light(begin, [steps[3]])
    line = light.line(0, [steps[4]])

    moved = sent_by(tokens, CORE | ZL, zl_is_not_core)
    state, a = first_rows(scal, tokens, moved, small)
    grad, g, sums_above = grad_rows(scal, grad_out, sent_by(grad_out, CORE | ZL, zl_is_not_core))

    wave = Heavy(line, [steps[5]])
    later = Light(tied(later, wave.halves))
    feed_places = {"u": (0, f), "d": (f, f)}
    attn_places = {n: (j * h, h) for j, n in enumerate("qkvo")}
    attn_weights, feed_weights = [], []

    saved = []
    for index in range(layers):
        attn_weights.append(Bundle(wave.lines(), 4, attn_places))
        line = light.line(1, [*wave.across, a])
        if index:
            g_rows = gathered_rows(g)
        a_other = swapped(a, CORE)
        mine, theirs, qkv, probs, mixed = attention(
            attn_weights[index], index, scal, a, a_other, small, [line] if index else [line, *later.halves]
        )
        middle, b = joined(
            state,
            [mine, swapped(theirs, CORE)],
            small,
            [index * ROWS + k for k in (4, 1, 3)],
            g_rows if index else [g],
        )
        b_rows = gathered_rows(b)
        wave = Heavy(line, [b])
        feed_weights.append(Bundle(wave.lines(), 2, feed_places))
        deps = () if index else later.across
        far = feed(feed_weights[index], index, scal, *b_rows[2:], small, deps)
        deps = far[1:2]
        if index == layers - 1:
            far_back = feed_back(feed_weights[index], scal, *g_rows[2:], far[3])
            deps = far_back[1:2]
        near = feed(feed_weights[index], index, scal, *b_rows[:2], small, deps)
        if index < layers - 1:
            light = later
            next_wave = Heavy(light.line(0, wave.across))
        active, slope = (near[2], far[2]), (near[3], far[3])
        saved.append((state, a, a_other, qkv, probs, mixed, middle, b_rows, active, slope))
        if index < layers - 1:
            wave = next_wave
            state, a = joined(
                middle,
                [near[0], swapped(near[1], CORE), from_far(far[0], far[1])],
                small,
                [index * ROWS + 5, (index + 1) * ROWS, (index + 1) * ROWS + 2],
            )
    last_near, last_far = near, far

    small_parts = [None] * layers
    feed_sums, attn_sums = [None] * layers, [None] * layers
    for index in reversed(range(layers)):
        state, a, a_other, qkv, probs, mixed, middle, b_rows, active, slope = saved[index]
        attn_w, feed_w = attn_weights[index], feed_weights[index]
        last = index == layers - 1
        if not last:
            g_rows = gathered_rows(g)
        near = feed_back(feed_w, scal, *g_rows[:2], slope[0])
        far = far_back if last else feed_back(feed_w, scal, *g_rows[2:], slope[1], near[1:2])
        fold = folded(far[0], far[1])
        *pieces, up_sum = weight_grads(
            feed_w,
            scal,
            [("d", 0, 0, 0, 2 * f), ("u", 1, 1, 0, 2 * f)],
            [g_rows, b_rows],
            [active, (near[2], far[2])],
            [0],
            [1],
            [fold] if last else [fold, *attn_sums[index + 1].a()],
        )
        feed_sums[index] = Reduction(pieces)
        deps = pieces[:1]
        if not last:
            deps = [*deps, *feed_sums[index + 1].b()]
        grad_mid, d, sums_two = norm_back(
            grad,
            middle,
            [near[0], swapped(near[1], CORE), swapped(fold, Z_MASK)],
            small,
            index * ROWS + 1,
            deps,
        )
        d_other = swapped(d, CORE)
        deps = () if last else [*feed_sums[index + 1].c(), *attn_sums[index + 1].b()]
        mine, theirs, triple = attention_back(attn_w, scal, d, d_other, qkv, probs, deps)
        moved = swapped(theirs, CORE)
        passed = feed_sums[index].a([moved])

        def chain(deps):
            return norm_back(grad_mid, state, [mine, moved], small, index * ROWS, deps)

        if last:
            grad, g, sums_one = chain(passed)
        *pieces, head_sum = weight_grads(
            attn_w,
            scal,
            [("q", 0, 0, 0, 4 * h), ("k", 0, 0, 4 * h, 4 * h), ("v", 0, 0, 8 * h, 4 * h)]
            + [("o", 1, 1, 0, 4 * h)],
            [(a, a_other), (d, d_other)],
            [(triple,), (mixed,)],
            [1],
            [0],
            [g] if last else [outcome, *feed_sums[index + 1].d()],
        )
        attn_sums[index] = Reduction(pieces)
        if last:
            outcome = joined(
                middle,
                [
                    last_near[0],
                    swapped(tied(last_near[1], [d]), CORE),
                    from_far(last_far[0], tied(last_far[1], [d])),
                ],
                small,
                [index * ROWS + 5, index * ROWS, index * ROWS + 2],
            )[0]
            activations = last_rows(scal, outcome)
        else:
            grad, g, sums_one = chain(pieces[:1])
        small_parts[index] = [sums_one, sums_two, sums_above, head_sum, up_sum]
        sums_above = sums_one
    input_grad = last_rows(scal, grad)
    small = summed_over(packed(scal, small_parts), [CORE])

    final, above = attn_sums
    final.a([*above.c(), *feed_sums[0].b(), grad])
    small = summed_over(tied(small, final.passed[:1]), [Z_MASK, ZL])
    final.b([input_grad, activations, small], True)
    feed_sums[0].c(final.parts[:1])
    moved = final.spread()
    steps, small = reduced_small(tied(small, moved[:1]), lane, own_wide)
    final.direct(moved, [*feed_sums[0].d(), *above.d(), steps[0]])
    ends = reduced_end(
        [a.total for a in attn_sums], [a.total for a in feed_sums], scal, steps[1:2], steps[2:3]
    )
    small = small.reshape(layers, ROWS, -1)
    qkv, out, up, down = call(
        result_kernel,
        [shape(w.shape, F32) for w in row_weights],
        [SMEM] + [VMEM] * 2,
        [scal, *ends],
        deps=[small],
    )
    return (
        activations,
        input_grad,
        qkv.transpose(0, 2, 1, 3),
        out.transpose(0, 2, 1),
        up,
        down.transpose(0, 2, 1),
        small[:, :2],
        small[:, 2:],
    )


def result_kernel(scal, mine, moved, qkv, out, up, down):
    grads = jnp.where(scal[1] != 0, mine[...], moved[...].astype(F32))
    wide, hidden = qkv.shape[3], up.shape[2]
    for layer in range(2):
        at = 4 * wide * layer
        for k in range(3):
            qkv[layer, k] = grads[:, at + k * wide : at + (k + 1) * wide]
        out[layer] = grads[:, at + 3 * wide : at + 4 * wide]
        at = 8 * wide + 2 * hidden * layer
        up[layer] = grads[:, at : at + hidden]
        down[layer] = grads[:, at + hidden : at + 2 * hidden]


def end_kernel(attns, *refs):
    *parts, near, far = refs
    at = 0
    for part in parts[:attns]:
        wide = part.shape[1] // 2
        near[:, at : at + wide] = part[:, :wide]
        far[:, at : at + wide] = part[:, wide:]
        at += wide
    for part in parts[attns:]:
        near[:, at : at + part.shape[1]] = part[...]
        at += part.shape[1]


def end_sum_kernel(scal, near, by_zl, by_zh, by_both, mine, theirs):
    rows = mine.shape[0]
    wide = by_zh.shape[1]
    for core, out in ((scal[2], mine), (1 - scal[2], theirs)):
        cut = pl.ds(pl.multiple_of(core * rows, rows), rows)
        total = near[cut, :].astype(F32) + by_zl[cut, :].astype(F32)
        attn = total[:, :wide] + (by_zh[cut, :].astype(F32) + by_both[cut, :].astype(F32))
        out[:, :wide] = attn.astype(out.dtype)
        out[:, wide:] = total[:, wide:].astype(out.dtype)


def reduced_end(attns, feeds, scal, deps=(), later=()):
    rows, wide = attns[0].shape[0], sum(a.shape[1] // 2 for a in attns)
    whole = wide + sum(f.shape[1] for f in feeds)
    near, far = call(
        functools.partial(end_kernel, len(attns)),
        [shape((rows, whole), BF), shape((rows, wide), BF)],
        [VMEM] * (len(attns) + len(feeds)),
        [*attns, *feeds],
        deps=deps,
    )
    mine, theirs = call(
        end_sum_kernel,
        [shape((rows // 2, whole), F32), shape((rows // 2, whole), BF)],
        [SMEM] + [VMEM] * 4,
        [
            scal,
            near,
            sent_by(near, ZL, zl_is_not_core),
            sent_by(far, ZH, zl_is_core),
            sent_by(far, Z_MASK, zl_is_not_core),
        ],
        deps=later,
    )
    return mine, sent_by(theirs, CORE, zl_is_core)


def solution(mesh):
    in_specs = (
        P(("dp", "tensor"), None),
        P("dp"),
        P(None, "dp", None, "tensor"),
        P(None, "tensor", "dp"),
        P(None, "dp", "tensor"),
        P(None, "tensor", "dp"),
        P(None, None, ("dp", "tensor")),
        P(None, None, ("dp", "tensor")),
        P(("dp", "tensor"), None),
    )
    out_specs = (
        P(("dp", "tensor"), None),
        P(("dp", "tensor"), None),
        P(None, "dp", None, "tensor"),
        P(None, "tensor", "dp"),
        P(None, "dp", "tensor"),
        P(None, "tensor", "dp"),
        P(None, None, ("dp", "tensor")),
        P(None, None, ("dp", "tensor")),
    )
    return jax.shard_map(
        per_device, mesh=mesh, in_specs=in_specs, out_specs=out_specs, check_vma=False
    )
```

```python
import functools
import math

import jax
import jax.numpy as jnp
from jax import lax
from jax.experimental import pallas as pl
from jax.experimental.pallas import tpu as pltpu
from jax.sharding import PartitionSpec as P

HEAD = 64
BUFFER = 64
EPS = 1e-06
NEG = -1e30
BF = jnp.bfloat16
F32 = jnp.float32
LANES = 128
ROWS = 12
FLOPS_PER_US = 1.15e9

PLACES = ("dp", "tensor")
DEVICES = 128
X_MASKS = (32, 64, 96)
YH, CORE, YL, ZH, ZL = 16, 8, 4, 2, 1
Y_MASKS = (YL, YH, YH | YL)
Z_MASK = ZH | ZL

ANY = pl.BlockSpec(memory_space=pl.ANY)
HBM = pl.BlockSpec(memory_space=pltpu.HBM)
VMEM = pl.BlockSpec(memory_space=pltpu.VMEM)
SMEM = pl.BlockSpec(memory_space=pltpu.SMEM)
WINDOW = pl.BlockSpec()


def swapped(array, mask):
    return lax.ppermute(array, PLACES, [(i, i ^ mask) for i in range(DEVICES)])


def sent_by(array, mask, sends):
    return lax.ppermute(array, PLACES, [(i, i ^ mask) for i in range(DEVICES) if sends(i)])


def zl_is_core(place):
    return place & ZL == (place & CORE) // CORE


def zl_is_not_core(place):
    return not zl_is_core(place)


def dot(left, right):
    return jnp.dot(left, right, preferred_element_type=F32)


def dot_turned(left, right):
    return lax.dot_general(left, right, (((1,), (1,)), ((), ())), preferred_element_type=F32)


def outer(left, right):
    return lax.dot_general(left, right, (((0,), (0,)), ((), ())), preferred_element_type=F32)


def call(body, outs, in_specs, args, scratch=(), out_specs=None, limit=12, deps=(), cost=0.5):
    out_specs = tuple(out_specs or [VMEM] * len(outs))
    outs = [
        pltpu.HBM(o.shape, o.dtype) if spec is WINDOW else o
        for o, spec in zip(outs, out_specs)
    ]
    args = [
        pltpu.with_memory_space_constraint(a, pltpu.HBM) if spec is WINDOW else a
        for a, spec in zip(args, in_specs)
    ]
    inputs = len(args)

    def kernel(*refs):
        body(*refs[:inputs], *refs[inputs + len(deps) :])

    windowed = any(spec.block_shape is not None for spec in in_specs)
    return pl.pallas_call(
        kernel,
        grid=(1,) if windowed else (),
        out_shape=tuple(outs),
        in_specs=[*in_specs, *[ANY] * len(deps)],
        out_specs=out_specs,
        scratch_shapes=list(scratch),
        compiler_params=pltpu.CompilerParams(vmem_limit_bytes=limit << 20),
        cost_estimate=pl.CostEstimate(
            flops=int(cost * FLOPS_PER_US), bytes_accessed=1, transcendentals=0
        ),
    )(*args, *deps)


def shape(dims, dtype):
    return jax.ShapeDtypeStruct(tuple(dims), dtype)


def bundle_scratch(wide):
    return pltpu.VMEM((4, 2, LANES, 2 * wide), BF)


def line_piece(lines, last, first):
    if last == 2:
        return lines[2 + first // 2].at[first % 2]
    return lines[(0, 1, None, 4)[last]].at[first]


def bundle_copies(core, wide, lines, whole, sems, inward):
    made = []
    for last in range(4):
        for first in range(4):
            x = last + core * (first - last)
            y = first + core * (last - first)
            at = pl.multiple_of((y % 2) * wide, LANES)
            ends = (line_piece(lines, last, first), whole.at[x, y // 2, :, pl.ds(at, wide)])
            made.append(
                pltpu.make_async_copy(*(ends if inward else ends[::-1]), sems.at[4 * last + first])
            )
    return made


def along(array, number, last):
    masks = (X_MASKS, Y_MASKS) if last else (Y_MASKS, X_MASKS)
    pairs = [
        (i, i ^ masks[1 if i & CORE else 0][number - 1]) for i in range(DEVICES)
    ]
    return lax.ppermute(array, PLACES, pairs)


def shard_kernel(w_qkv, w_out, w_up, w_down, out):
    wide, hidden = w_qkv.shape[3], w_up.shape[2]
    for layer in range(2):
        at = 4 * wide * layer
        for k in range(3):
            out[:, at + k * wide : at + (k + 1) * wide] = w_qkv[layer, k]
        out[:, at + 3 * wide : at + 4 * wide] = w_out[layer]
        at = 8 * wide + 2 * hidden * layer
        out[:, at : at + hidden] = w_up[layer]
        out[:, at + hidden : at + 2 * hidden] = w_down[layer]


def both_kernel(scal, mine, other, out):
    rows = mine.shape[0]
    out[pl.ds(pl.multiple_of(scal[2] * rows, rows), rows), :] = mine[...]
    out[pl.ds(pl.multiple_of((1 - scal[2]) * rows, rows), rows), :] = other[...]


def begin_kernel(layer, scal, both, by_zl, by_zh, by_both, out):
    mine = scal[1] != 0
    attn = by_zh.shape[1] // 2
    feed = by_zl.shape[1] - attn
    cols = slice(attn * layer, attn * (layer + 1))
    rest = slice(2 * attn + feed * layer, 2 * attn + feed * (layer + 1))
    out[:, :attn] = jnp.where(mine, both[:, cols], by_zl[:, :attn])
    out[:, attn : 2 * attn] = jnp.where(mine, by_zh[:, cols], by_both[:, cols])
    out[:, 2 * attn :] = jnp.where(mine, both[:, rest], by_zl[:, attn:])


def cores_joined(shard, scal, deps):
    return call(
        both_kernel,
        [shape((2 * shard.shape[0], shard.shape[1]), BF)],
        [SMEM, VMEM, VMEM],
        [scal, shard, swapped(shard, CORE)],
        deps=deps,
    )[0]


def begun(both, scal, attn, deps=()):
    feed = both.shape[1] // 2 - attn
    part = both[:, : 2 * attn]
    far = [sent_by(part, m, zl_is_core) for m in (ZH, Z_MASK)]
    outs = []
    for layer in range(2):
        first = 2 * attn + feed * layer
        cols = (both[:, attn * layer : attn * (layer + 1)], both[:, first : first + feed])
        near = sent_by(jnp.concatenate(cols, axis=1), ZL, zl_is_core)
        outs.append(
            call(
                functools.partial(begin_kernel, layer),
                [shape((both.shape[0], 2 * attn + feed), BF)],
                [SMEM] + [VMEM] * 4,
                [scal, both, near, *far],
                deps=() if layer else deps,
            )[0]
        )
    return outs


def block(array, axis, at, parts):
    dims = tuple(n // parts if k == axis else n for k, n in enumerate(array.shape))
    place = tuple(at if k == axis else 0 for k in range(array.ndim))
    return pl.BlockSpec(dims, lambda *_: place), dims


def copies_kernel(*refs):
    half = len(refs) // 2
    for source, out in zip(refs[:half], refs[half:]):
        out[...] = source[...]


def halves_of(near, far, deps=(), axis=0):
    specs = [block(near, axis, 0, 2), block(far, axis, 1, 2)]
    return call(
        copies_kernel,
        [shape(dims, BF) for _, dims in specs],
        [spec for spec, _ in specs],
        [near, far],
        deps=deps,
    )


def line_kernel(*refs):
    for k in range(4):
        refs[4][k] = refs[k][...]


class Light:
    def __init__(self, begin, deps=()):
        self.begin = begin
        self.near, self.far = along(begin, 1, False), along(begin, 3, False)
        self.halves = halves_of(self.near, self.far, deps, 1)
        one, two = self.halves
        self.across = [along(one, 3, False), along(two, 1, False)]

    def line(self, k, deps=()):
        specs = [block(a, 1, k, 2) for a in (self.begin, self.near, self.far)]
        across = self.across[k]
        specs.insert(2, (VMEM, across.shape))
        return call(
            line_kernel,
            [shape((4, *across.shape), BF)],
            [spec for spec, _ in specs],
            [self.begin, self.near, across, self.far],
            deps=deps,
        )[0]


def tie_kernel(*refs):
    refs[-1][...] = refs[0][...]


def tied(array, deps):
    return call(tie_kernel, [shape(array.shape, array.dtype)], [VMEM], [array], deps=deps)[0]


class Heavy:
    def __init__(self, line, deps=()):
        self.line = line
        self.near, self.far = along(line, 1, True), along(line, 3, True)
        self.halves = halves_of(self.near, self.far, deps)
        one, two = self.halves
        self.across = [along(one, 3, True), along(two, 1, True)]

    def lines(self):
        return [self.line, self.near, *self.across, self.far]


def sum_kernel(count, *refs):
    total = refs[0][...].astype(F32)
    for ref in refs[1:count]:
        total = total + ref[...].astype(F32)
    total = total.astype(BF)
    outs = refs[count:]
    if len(outs) == 1:
        outs[0][...] = total
        return
    if len(outs) == 4:
        for k, out in enumerate(outs):
            out[...] = total[k]
        return
    keep, send = outs
    for k in range(2):
        keep[k] = total[k]
        send[k] = total[3 - k]


def halves_kernel(keep, moved, mine, send):
    total = (keep[...].astype(F32) + moved[...].astype(F32)).astype(BF)
    mine[...] = total[0]
    send[...] = total[1]


def summed(arrays, outs, deps=()):
    return call(
        functools.partial(sum_kernel, len(arrays)),
        outs,
        [VMEM] * len(arrays),
        arrays,
        deps=deps,
    )


def pass_on_kernel(near, far, to_far, to_near, near_out, far_out):
    half = near.shape[0] // 2
    near_out[:half] = near[:half]
    near_out[half:] = (near[half:].astype(F32) + to_near[...].astype(F32)).astype(BF)
    far_out[:half] = (far[:half].astype(F32) + to_far[...].astype(F32)).astype(BF)
    far_out[half:] = far[half:]


class Reduction:
    def __init__(self, lines):
        self.lines = lines

    def a(self, deps=()):
        mine, near, across_one, across_two, far = self.lines
        moved = [along(across_one, 1, True), along(across_two, 3, True)]
        self.passed = call(
            pass_on_kernel,
            [shape(near.shape, BF)] * 2,
            [VMEM] * 4,
            [near, far, *moved],
            deps=deps,
        )
        return self.passed[:1]

    def b(self, deps=(), direct=False):
        near, far = self.passed
        mine = self.lines[0]
        outs = [shape((2, *mine.shape[1:]), BF)] * 2
        if direct:
            outs = [shape(mine.shape[1:], BF)] * 4
        self.parts = summed([mine, along(near, 1, True), along(far, 3, True)], outs, deps)
        return self.parts[:1]

    def c(self, deps=()):
        keep, send = self.parts
        outs = [shape(keep.shape[1:], BF)] * 2
        self.pair = call(
            halves_kernel, outs, [VMEM] * 2, [keep, along(send, 3, False)], deps=deps
        )
        return self.pair[:1]

    def spread(self):
        return [along(self.parts[k], k, False) for k in (1, 2, 3)]

    def direct(self, moved, deps=()):
        outs = [shape(moved[0].shape, BF)]
        self.total = summed([self.parts[0], *moved], outs, deps)[0]

    def d(self, deps=()):
        mine, send = self.pair
        outs = [shape(mine.shape, BF)]
        self.total = summed([mine, along(send, 1, False)], outs, deps)[0]
        return [self.total]


class Bundle:
    def __init__(self, lines, blocks, places):
        self.lines = lines
        self.blocks = blocks
        self.wide = lines[0].shape[2]
        self.step = 2 * self.wide // blocks
        self.places = places

    def scratch(self):
        return [bundle_scratch(self.wide), pltpu.SemaphoreType.DMA((16,))]

    def out_shapes(self):
        return [shape(l.shape, BF) for l in self.lines]

    def copies(self, core, refs, scratch, inward):
        return bundle_copies(core, self.wide, refs, scratch[0], scratch[1], inward)

    def columns(self, scratch, name, blocks=None):
        first, wide = self.places[name]
        blocks = tuple(range(self.blocks)) if blocks is None else blocks
        cuts = [
            scratch[0][:, :, :, b * self.step + first : b * self.step + first + wide]
            for b in blocks
        ]
        whole = jnp.concatenate(cuts, axis=-1) if len(cuts) > 1 else cuts[0]
        return whole.reshape(-1, wide * len(blocks))

    def store(self, scratch, name, value, x):
        first, wide = self.places[name]
        value = value.reshape(2, LANES, -1)
        for b in range(self.blocks):
            scratch[0][x, :, :, b * self.step + first : b * self.step + first + wide] = value[
                :, :, b * wide : (b + 1) * wide
            ]


def start(copies):
    for copy in copies:
        copy.start()


def finish(copies):
    for copy in copies:
        copy.wait()


def both_rows(own, other):
    return jnp.concatenate([own[...], other[...]])


def lane_halves(value):
    lane = lax.broadcasted_iota(jnp.int32, value.shape, 1)
    zero = jnp.zeros_like(value)
    return jnp.where(lane < HEAD, value, zero), jnp.where(lane < HEAD, zero, value)


def attention_kernel(weights, layer, scal, own, other, small, *refs):
    pieces, refs = refs[:5], refs[5:]
    mine, theirs, qkv, probs, mixed = refs[:5]
    scratch = refs[5:]
    core, valid = scal[2], scal[3]
    copies = weights.copies(core, pieces, scratch, True)
    start(copies)
    rows = own.shape[0]
    seq = 2 * rows
    a = both_rows(own, other)
    finish(copies)
    wide = qkv.shape[1] // 3
    places = [
        pl.multiple_of(
            (((scal[4] ^ ylr) * 4 + (scal[5] ^ zhr) * 2 + core) ^ scal[0]) * LANES, LANES
        )
        for ylr in range(2)
        for zhr in range(2)
    ]
    for k, name in enumerate("qkv"):
        part = dot(a, weights.columns(scratch, name))
        if name != "k":
            at = layer * ROWS + (6 if name == "q" else 7)
            bias = [small[at : at + 1, pl.ds(place, LANES)] for place in places]
            part = part + jnp.concatenate(bias, axis=1)
        qkv[:, k * wide : (k + 1) * wide] = part.astype(BF)
    key = lax.broadcasted_iota(jnp.int32, (1, seq), 1)
    position = jnp.where(key < rows, key + core * rows, key - core * rows)
    allowed = position < valid
    factor = 1.0 / math.sqrt(HEAD)
    for b in range(wide // LANES):
        lanes = slice(b * LANES, (b + 1) * LANES)
        q = qkv[:, b * LANES : (b + 1) * LANES]
        k = qkv[:, wide + b * LANES : wide + (b + 1) * LANES]
        v = qkv[:, 2 * wide + b * LANES : 2 * wide + (b + 1) * LANES]
        total = None
        for h, (q_h, v_h) in enumerate(zip(lane_halves(q), lane_halves(v))):
            scores = jnp.where(allowed, dot_turned(q_h, k) * factor, NEG)
            expo = jnp.exp(scores - jnp.max(scores, axis=-1, keepdims=True))
            p = (expo / jnp.sum(expo, axis=-1, keepdims=True)).astype(BF)
            probs[2 * b + h] = p
            part = dot(p, v_h)
            total = part if total is None else total + part
        mixed[:, lanes] = total.astype(BF)
    out = dot_turned(mixed[...], weights.columns(scratch, "o"))
    mine[...] = out[:rows]
    theirs[...] = out[rows:].astype(BF)


def attention(weights, layer, scal, own, other, small, deps):
    rows, width = own.shape
    wide = width // 2
    seq = 2 * rows
    outs = [
        shape((rows, width), F32),
        shape((rows, width), BF),
        shape((seq, 3 * wide), BF),
        shape((wide // HEAD, seq, seq), BF),
        shape((seq, wide), BF),
    ]
    return call(
        functools.partial(attention_kernel, weights, layer),
        outs,
        [SMEM, VMEM, VMEM, VMEM] + [HBM] * 5,
        [scal, own, other, small, *weights.lines],
        weights.scratch(),
        out_specs=[VMEM, VMEM, WINDOW, WINDOW, WINDOW],
        deps=deps,
        cost=6.0,
    )


def attention_back_kernel(weights, scal, own, other, qkv, probs, *refs):
    pieces, refs = refs[:5], refs[5:]
    mine, theirs, grads = refs[:3]
    scratch = refs[3:]
    copies = weights.copies(scal[2], pieces, scratch, True)
    start(copies)
    rows = own.shape[0]
    wide = qkv.shape[1] // 3
    d = both_rows(own, other)
    finish(copies)
    factor = 1.0 / math.sqrt(HEAD)
    spread = dot(d, weights.columns(scratch, "o")).astype(BF)
    for b in range(wide // LANES):
        q = qkv[:, b * LANES : (b + 1) * LANES]
        k = qkv[:, wide + b * LANES : wide + (b + 1) * LANES]
        v = qkv[:, 2 * wide + b * LANES : 2 * wide + (b + 1) * LANES]
        do = spread[:, b * LANES : (b + 1) * LANES]
        dq = dk = dv = None
        parts = zip(lane_halves(q), lane_halves(k), lane_halves(do))
        for h, (q_h, k_h, do_h) in enumerate(parts):
            p = probs[2 * b + h]
            dv_h = outer(p, do_h)
            dp = dot_turned(do_h, v)
            wide_p = p.astype(F32)
            ds = wide_p * (dp - jnp.sum(wide_p * dp, axis=-1, keepdims=True))
            ds = ds.astype(BF)
            dq_h = dot(ds, k_h)
            dk_h = outer(ds, q_h)
            dq, dk, dv = (
                (dq_h, dk_h, dv_h) if dq is None else (dq + dq_h, dk + dk_h, dv + dv_h)
            )
        grads[:, b * LANES : (b + 1) * LANES] = (dq * factor).astype(BF)
        grads[:, wide + b * LANES : wide + (b + 1) * LANES] = (dk * factor).astype(BF)
        grads[:, 2 * wide + b * LANES : 2 * wide + (b + 1) * LANES] = dv.astype(BF)
    whole = jnp.concatenate([weights.columns(scratch, name) for name in "qkv"], axis=1)
    out = dot_turned(grads[...], whole)
    mine[...] = out[:rows]
    theirs[...] = out[rows:].astype(BF)


def attention_back(weights, scal, own, other, qkv, probs, deps=()):
    rows, width = own.shape
    seq, wide = qkv.shape[0], qkv.shape[1] // 3
    outs = [shape((rows, width), F32), shape((rows, width), BF), shape(qkv.shape, BF)]
    return call(
        functools.partial(attention_back_kernel, weights),
        outs,
        [SMEM, VMEM, VMEM, WINDOW, WINDOW] + [HBM] * 5,
        [scal, own, other, qkv, probs, *weights.lines],
        weights.scratch(),
        deps=deps,
        cost=7.0,
    )


def weight_grad_kernel(weights, jobs, lefts, rights, sums, scal, *refs):
    values = []
    for count in (*lefts, *rights):
        values.append(jnp.concatenate([r[...] for r in refs[:count]]) if count > 1 else refs[0])
        refs = refs[count:]
    pieces, refs = refs[:5], refs[5:]
    sum_refs, scratch = refs[: len(sums)], refs[len(sums) :]
    for name, left, right, first, wide in jobs:
        block = values[left].shape[1] // 4
        for x in range(4):
            grad = outer(
                values[left][:, x * block : (x + 1) * block],
                values[len(lefts) + right][:, first : first + wide],
            )
            weights.store(scratch, name, grad.astype(BF), x)
    copies = weights.copies(scal[2], pieces, scratch, False)
    start(copies)
    for ref, k in zip(sum_refs, sums):
        ref[...] = jnp.sum(values[len(lefts) + k][...].astype(F32), axis=0, keepdims=True)
    finish(copies)


def weight_grads(weights, scal, jobs, lefts, rights, kept, sums, deps=()):
    outs = weights.out_shapes() + [shape((1, rights[k][0].shape[1]), F32) for k in sums]
    arrays = [a for group in (*lefts, *rights) for a in group]
    rows = sum(a.shape[0] for a in lefts[0])
    return call(
        functools.partial(
            weight_grad_kernel,
            weights,
            jobs,
            [len(g) for g in lefts],
            [len(g) for g in rights],
            sums,
        ),
        outs,
        [SMEM]
        + [VMEM] * sum(len(g) for g in lefts)
        + [WINDOW if k in kept else VMEM for k, g in enumerate(rights) for _ in g],
        [scal, *arrays],
        weights.scratch(),
        out_specs=[HBM] * 5 + [VMEM] * len(sums),
        deps=deps,
        cost=5.0,
    )


def hidden_places(scal, layer, ylr):
    row = (scal[4] ^ ylr) * 2 + scal[5]
    mask = lax.broadcasted_iota(jnp.int32, (4, LANES), 0) == row
    return mask, [pl.multiple_of(((scal[2] * 4 + k) ^ scal[0]) * LANES, LANES) for k in range(4)]


def feed_kernel(weights, layer, scal, own, other, small, *refs):
    pieces, refs = refs[:5], refs[5:]
    mine, theirs, active, slope = refs[:4]
    scratch = refs[4:]
    copies = weights.copies(scal[2], pieces, scratch, True)
    start(copies)
    rows = own.shape[0]
    b = both_rows(own, other)
    finish(copies)
    wide = active.shape[1] // 2
    for k in range(2):
        cols = slice(k * wide, (k + 1) * wide)
        mask, places = hidden_places(scal, layer, k)
        at = layer * ROWS + 8
        bias = [jnp.where(mask, small[at : at + 4, pl.ds(p, LANES)], 0.0) for p in places]
        bias = jnp.sum(jnp.concatenate(bias, axis=1), axis=0, keepdims=True)
        u = dot(b, weights.columns(scratch, "u", (k,))) + bias
        below = 0.5 + 0.5 * lax.erf(u * math.sqrt(0.5))
        active[:, cols] = (u * below).astype(BF)
        bell = jnp.exp(u * u * -0.5) * (1.0 / math.sqrt(2.0 * math.pi))
        slope[:, cols] = (below + u * bell).astype(BF)
    out = dot_turned(active[...], weights.columns(scratch, "d"))
    mine[...] = out[:rows]
    theirs[...] = out[rows:].astype(BF)


def feed(weights, layer, scal, own, other, small, deps=()):
    rows, width = own.shape
    seq, wide = 2 * rows, width
    outs = [
        shape((rows, width), F32),
        shape((rows, width), BF),
        shape((seq, wide), BF),
        shape((seq, wide), BF),
    ]
    return call(
        functools.partial(feed_kernel, weights, layer),
        outs,
        [SMEM, VMEM, VMEM, VMEM] + [HBM] * 5,
        [scal, own, other, small, *weights.lines],
        weights.scratch(),
        out_specs=[VMEM, VMEM, WINDOW, WINDOW],
        deps=deps,
        cost=3.5,
    )


def feed_back_kernel(weights, scal, own, other, slope, *refs):
    pieces, refs = refs[:5], refs[5:]
    mine, theirs, grads = refs[:3]
    scratch = refs[3:]
    copies = weights.copies(scal[2], pieces, scratch, True)
    start(copies)
    rows = own.shape[0]
    g = both_rows(own, other)
    finish(copies)
    wide = slope.shape[1] // 2
    for k in range(2):
        cols = slice(k * wide, (k + 1) * wide)
        dz = dot(g, weights.columns(scratch, "d", (k,)))
        grads[:, cols] = (dz * slope[:, cols].astype(F32)).astype(BF)
    out = dot_turned(grads[...], weights.columns(scratch, "u"))
    mine[...] = out[:rows]
    theirs[...] = out[rows:].astype(BF)


def feed_back(weights, scal, own, other, slope, deps=()):
    rows, width = own.shape
    outs = [shape((rows, width), F32), shape((rows, width), BF), shape(slope.shape, BF)]
    return call(
        functools.partial(feed_back_kernel, weights),
        outs,
        [SMEM, VMEM, VMEM, WINDOW] + [HBM] * 5,
        [scal, own, other, slope, *weights.lines],
        weights.scratch(),
        deps=deps,
        cost=3.3,
    )


def in_order(ref, order):
    wide = ref.shape[1] // 8
    return jnp.concatenate(
        [ref[:, pl.ds(pl.multiple_of((k ^ order) * wide, wide), wide)] for k in range(8)], axis=1
    )


def normed(rows, gain, shift):
    centre = rows - jnp.mean(rows, axis=-1, keepdims=True)
    spread = jnp.mean(centre * centre, axis=-1, keepdims=True)
    return centre * lax.rsqrt(spread + EPS) * gain + shift


def first_kernel(scal, mine, moved, small, state, out):
    stays = scal[1] != 0
    order = scal[0]
    rows = jnp.where(stays, in_order(mine, order).astype(F32), in_order(moved, order).astype(F32))
    state[...] = rows
    out[...] = normed(rows, small[0:1], small[2:3]).astype(BF)


def first_rows(scal, mine, moved, small):
    outs = [shape(mine.shape, F32), shape(mine.shape, BF)]
    return call(
        first_kernel,
        outs,
        [SMEM] + [VMEM] * 3,
        [scal, mine, moved, small],
        out_specs=[WINDOW, VMEM],
    )


def grad_kernel(scal, mine, moved, state, out, sums):
    stays = scal[1] != 0
    order = scal[0]
    rows = jnp.where(stays, in_order(mine, order), in_order(moved, order))
    state[...] = rows
    out[...] = rows.astype(BF)
    sums[...] = jnp.sum(rows, axis=0, keepdims=True)


def grad_rows(scal, mine, moved):
    outs = [shape(mine.shape, F32), shape(mine.shape, BF), shape((1, mine.shape[1]), F32)]
    return call(grad_kernel, outs, [SMEM] + [VMEM] * 2, [scal, mine, moved])


def last_kernel(scal, mine, moved, out):
    stays = scal[1] != 0
    order = scal[0]
    out[...] = jnp.where(stays, in_order(mine, order), in_order(moved, order))


def last_rows(scal, mine):
    moved = sent_by(mine, CORE | ZL, zl_is_not_core)
    return call(
        last_kernel, [shape(mine.shape, F32)], [SMEM] + [VMEM] * 2, [scal, mine, moved]
    )[0]


def total_of(refs):
    total = refs[0][...].astype(F32)
    for ref in refs[1:]:
        total = total + ref[...].astype(F32)
    return total


def join_kernel(at, rows, small, *refs):
    *parts, state, out = refs
    bias, gain, shift = (small[k : k + 1] for k in at)
    total = rows[...] + (total_of(parts) + bias)
    state[...] = total
    out[...] = normed(total, gain, shift).astype(BF)


def joined(rows, parts, small, at, deps=()):
    outs = [shape(rows.shape, F32), shape(rows.shape, BF)]
    return call(
        functools.partial(join_kernel, at),
        outs,
        [WINDOW, VMEM] + [VMEM] * len(parts),
        [rows, small, *parts],
        out_specs=[WINDOW, VMEM],
        deps=deps,
        cost=2.0,
    )


def norm_back_kernel(at, above, rows, small, *refs):
    *parts, state, out, sums = refs
    dy = total_of(parts)
    centre = rows[...] - jnp.mean(rows[...], axis=-1, keepdims=True)
    scale = lax.rsqrt(jnp.mean(centre * centre, axis=-1, keepdims=True) + EPS)
    unit = centre * scale
    weighed = dy * small[at : at + 1]
    inner = weighed - jnp.mean(weighed, axis=-1, keepdims=True)
    inner = inner - unit * jnp.mean(weighed * unit, axis=-1, keepdims=True)
    total = above[...] + inner * scale
    state[...] = total
    out[...] = total.astype(BF)
    sums[0:1] = jnp.sum(dy * unit, axis=0, keepdims=True)
    sums[1:2] = jnp.sum(dy, axis=0, keepdims=True)
    sums[2:3] = jnp.sum(total, axis=0, keepdims=True)


def norm_back(above, rows, parts, small, at, deps=()):
    outs = [shape(rows.shape, F32), shape(rows.shape, BF), shape((3, rows.shape[1]), F32)]
    return call(
        functools.partial(norm_back_kernel, at),
        outs,
        [VMEM, WINDOW, VMEM] + [VMEM] * len(parts),
        [above, rows, small, *parts],
        deps=deps,
        cost=1.7,
    )


def fold_kernel(mine, theirs, out):
    out[...] = (mine[...] + theirs[...].astype(F32)).astype(BF)


def folded(mine, theirs, deps=()):
    moved = swapped(theirs, CORE)
    return call(fold_kernel, [shape(mine.shape, BF)], [VMEM] * 2, [mine, moved], deps=deps)[0]


def from_far(mine, theirs):
    return swapped(folded(mine, theirs), Z_MASK)


def gathered_rows(own):
    far = swapped(own, Z_MASK)
    return own, swapped(own, CORE), far, swapped(far, CORE)


def gathered_small(small, lane):
    part = jnp.zeros((small.shape[0], LANES), F32)
    part = lax.dynamic_update_slice(part, small, (0, lane))
    steps = [part + swapped(part, YL)]
    for mask in (YH | YL, X_MASKS[0]):
        steps.append(jnp.concatenate([steps[-1], swapped(steps[-1], mask)], axis=1))
    half = steps[-1].shape[1] // 2
    moved = swapped(steps[-1], X_MASKS[2])
    steps.append(jnp.concatenate([steps[-1], moved[:, half:], moved[:, :half]], axis=1))
    for mask in (CORE, Z_MASK, ZL):
        steps.append(steps[-1] + swapped(steps[-1], mask))
    return steps


def summed_over(small, masks):
    for mask in masks:
        small = small + swapped(small, mask)
    return small


def reduced_small(small, lane, wide):
    steps = []
    half = small.shape[1] // 2
    quarter = half // 2
    send = jnp.concatenate([small[:, half + quarter :], small[:, half : half + quarter]], axis=1)
    steps.append(small[:, :half] + swapped(send, X_MASKS[2]))
    for mask in (X_MASKS[0], YH | YL):
        half = steps[-1].shape[1] // 2
        steps.append(steps[-1][:, :half] + swapped(steps[-1][:, half:], mask))
    small = summed_over(steps[-1], [YL])
    return steps, lax.dynamic_slice(small, (0, lane), (small.shape[0], wide))


def pack_kernel(layers, scal, *refs):
    out = refs[-1]
    out[...] = jnp.zeros(out.shape, F32)
    for layer in range(layers):
        one, two, above, heads, hidden = refs[5 * layer : 5 * layer + 5]
        at = layer * ROWS
        out[at : at + 1] = one[0:1]
        out[at + 1 : at + 2] = two[0:1]
        out[at + 2 : at + 3] = one[1:2]
        out[at + 3 : at + 4] = two[1:2]
        out[at + 4 : at + 5] = two[2:3]
        out[at + 5 : at + 6] = above[above.shape[0] - 1 : above.shape[0]]
        wide = heads.shape[1] // 3
        for k in range(4):
            block = (scal[4] ^ (k // 2)) * 4 + (scal[5] ^ (k % 2)) * 2 + scal[2]
            place = pl.multiple_of((block ^ scal[0]) * LANES, LANES)
            for row, first in ((6, 0), (7, 2 * wide)):
                first += k * LANES
                out[at + row : at + row + 1, pl.ds(place, LANES)] = heads[:, first : first + LANES]
        for ylr in range(2):
            mask, places = hidden_places(scal, layer, ylr)
            for k, place in enumerate(places):
                first = (4 * ylr + k) * LANES
                part = jnp.where(mask, hidden[:, first : first + LANES], 0.0)
                out[at + 8 : at + 12, pl.ds(place, LANES)] += part


def packed(scal, parts):
    arrays = [a for layer in parts for a in layer]
    out = shape((ROWS * len(parts), arrays[0].shape[1]), F32)
    return call(
        functools.partial(pack_kernel, len(parts)), [out], [SMEM] + [VMEM] * len(arrays), [scal, *arrays]
    )[0]


def per_device(tokens, kept, w_qkv, w_out, w_up, w_down, ln_gains, biases, grad_out):
    dp_place = lax.axis_index("dp")
    tensor_place = lax.axis_index("tensor")
    core = dp_place % 2
    order = dp_place // 2
    yl = tensor_place // 4
    zh = (tensor_place // 2) % 2
    zl = tensor_place % 2
    rows, width = tokens.shape
    layers = w_qkv.shape[0]
    head_wide = w_qkv.shape[3]
    hidden_wide = w_up.shape[2]

    both_kept = jnp.where(zl == core, kept, swapped(kept, CORE))
    valid = BUFFER + lax.dynamic_index_in_dim(both_kept, yl * 2 + zh, keepdims=False)
    scal = jnp.stack(
        [order, (zl == core).astype(jnp.int32), core, valid.astype(jnp.int32), yl, zh, zl]
    ).astype(jnp.int32)
    own_wide = ln_gains.shape[2]
    lane = (core * 8 + tensor_place) * own_wide

    h, f = head_wide, hidden_wide

    row_weights = [
        w_qkv.transpose(0, 2, 1, 3),
        w_out.transpose(0, 2, 1),
        w_up,
        w_down.transpose(0, 2, 1),
    ]

    shard = call(
        shard_kernel,
        [shape((w_up.shape[1], 8 * h + 4 * f), BF)],
        [WINDOW] * 4,
        row_weights,
    )[0]
    small = jnp.concatenate([ln_gains, biases], axis=1).reshape(layers * ROWS, own_wide)
    steps = gathered_small(tied(small, [shard]), lane)
    small = steps[-1]

    both = cores_joined(shard, scal, ())
    begin, later = begun(both, scal, 4 * h, [steps[2]])
    light = Light(begin, [steps[3]])
    line = light.line(0, [steps[4]])

    moved = sent_by(tokens, CORE | ZL, zl_is_not_core)
    state, a = first_rows(scal, tokens, moved, small)
    grad, g, sums_above = grad_rows(scal, grad_out, sent_by(grad_out, CORE | ZL, zl_is_not_core))

    wave = Heavy(line, [steps[5]])
    later = Light(tied(later, wave.halves))
    feed_places = {"u": (0, f), "d": (f, f)}
    attn_places = {n: (j * h, h) for j, n in enumerate("qkvo")}
    attn_weights, feed_weights = [], []

    saved = []
    for index in range(layers):
        attn_weights.append(Bundle(wave.lines(), 4, attn_places))
        line = light.line(1, [*wave.across, a])
        if index:
            g_rows = gathered_rows(g)
        a_other = swapped(a, CORE)
        mine, theirs, qkv, probs, mixed = attention(
            attn_weights[index], index, scal, a, a_other, small, [line] if index else [line, *later.halves]
        )
        middle, b = joined(
            state,
            [mine, swapped(theirs, CORE)],
            small,
            [index * ROWS + k for k in (4, 1, 3)],
            g_rows if index else [g],
        )
        b_rows = gathered_rows(b)
        wave = Heavy(line, [b])
        feed_weights.append(Bundle(wave.lines(), 2, feed_places))
        deps = () if index else later.across
        far = feed(feed_weights[index], index, scal, *b_rows[2:], small, deps)
        deps = far[1:2]
        if index == layers - 1:
            far_back = feed_back(feed_weights[index], scal, *g_rows[2:], far[3])
            deps = far_back[1:2]
        near = feed(feed_weights[index], index, scal, *b_rows[:2], small, deps)
        if index < layers - 1:
            light = later
            next_wave = Heavy(light.line(0, wave.across))
        active, slope = (near[2], far[2]), (near[3], far[3])
        saved.append((state, a, a_other, qkv, probs, mixed, middle, b_rows, active, slope))
        if index < layers - 1:
            wave = next_wave
            state, a = joined(
                middle,
                [near[0], swapped(near[1], CORE), from_far(far[0], far[1])],
                small,
                [index * ROWS + 5, (index + 1) * ROWS, (index + 1) * ROWS + 2],
            )
    last_near, last_far = near, far

    small_parts = [None] * layers
    feed_sums, attn_sums = [None] * layers, [None] * layers
    for index in reversed(range(layers)):
        state, a, a_other, qkv, probs, mixed, middle, b_rows, active, slope = saved[index]
        attn_w, feed_w = attn_weights[index], feed_weights[index]
        last = index == layers - 1
        if not last:
            g_rows = gathered_rows(g)
        near = feed_back(feed_w, scal, *g_rows[:2], slope[0])
        far = far_back if last else feed_back(feed_w, scal, *g_rows[2:], slope[1], near[1:2])
        fold = folded(far[0], far[1], () if last else feed_sums[index + 1].b())
        *pieces, up_sum = weight_grads(
            feed_w,
            scal,
            [("d", 0, 0, 0, 2 * f), ("u", 1, 1, 0, 2 * f)],
            [g_rows, b_rows],
            [active, (near[2], far[2])],
            [0],
            [1],
            [fold] if last else [fold, *attn_sums[index + 1].a([fold])],
        )
        feed_sums[index] = Reduction(pieces)
        deps = pieces[:1]
        grad_mid, d, sums_two = norm_back(
            grad,
            middle,
            [near[0], swapped(near[1], CORE), swapped(fold, Z_MASK)],
            small,
            index * ROWS + 1,
            deps,
        )
        d_other = swapped(d, CORE)
        deps = () if last else [*attn_sums[index + 1].b(), last_fold]
        mine, theirs, triple = attention_back(attn_w, scal, d, d_other, qkv, probs, deps)
        moved = swapped(theirs, CORE)
        passed = feed_sums[index].a([moved])

        def chain(deps):
            return norm_back(grad_mid, state, [mine, moved], small, index * ROWS, deps)

        if last:
            grad, g, sums_one = chain(passed)
        *pieces, head_sum = weight_grads(
            attn_w,
            scal,
            [("q", 0, 0, 0, 4 * h), ("k", 0, 0, 4 * h, 4 * h), ("v", 0, 0, 8 * h, 4 * h)]
            + [("o", 1, 1, 0, 4 * h)],
            [(a, a_other), (d, d_other)],
            [(triple,), (mixed,)],
            [1],
            [0],
            [g] if last else feed_sums[index + 1].c(),
        )
        attn_sums[index] = Reduction(pieces)
        if last:
            last_fold = folded(last_far[0], tied(last_far[1], [d]))
            outcome = joined(
                middle,
                [
                    last_near[0],
                    swapped(tied(last_near[1], [d]), CORE),
                    swapped(last_fold, Z_MASK),
                ],
                small,
                [index * ROWS + 5, index * ROWS, index * ROWS + 2],
            )[0]
            activations = last_rows(scal, outcome)
        else:
            grad, g, sums_one = chain(pieces[:1])
        small_parts[index] = [sums_one, sums_two, sums_above, head_sum, up_sum]
        sums_above = sums_one
    input_grad = last_rows(scal, grad)
    small = summed_over(packed(scal, small_parts), [CORE])

    final, above = attn_sums
    final.a([*above.c(), *feed_sums[0].b(), grad, outcome])
    final.b([activations, input_grad, small], True)
    feed_sums[0].c(final.parts[:1])
    moved = final.spread()
    small = summed_over(tied(small, moved[:1]), [Z_MASK, ZL])
    final.direct(moved, [*feed_sums[0].d(), *above.d(), *feed_sums[1].d()])
    steps, small_sums = reduced_small(small, lane, own_wide)
    ends = reduced_end(
        [a.total for a in attn_sums], [a.total for a in feed_sums], scal, [small], steps[2:3]
    )
    small = small_sums
    small = small.reshape(layers, ROWS, -1)
    qkv, out, up, down = call(
        result_kernel,
        [shape(w.shape, F32) for w in row_weights],
        [SMEM] + [VMEM] * 2,
        [scal, *ends],
        deps=[small],
    )
    return (
        activations,
        input_grad,
        qkv.transpose(0, 2, 1, 3),
        out.transpose(0, 2, 1),
        up,
        down.transpose(0, 2, 1),
        small[:, :2],
        small[:, 2:],
    )


def result_kernel(scal, mine, moved, qkv, out, up, down):
    grads = jnp.where(scal[1] != 0, mine[...], moved[...].astype(F32))
    wide, hidden = qkv.shape[3], up.shape[2]
    for layer in range(2):
        at = 4 * wide * layer
        for k in range(3):
            qkv[layer, k] = grads[:, at + k * wide : at + (k + 1) * wide]
        out[layer] = grads[:, at + 3 * wide : at + 4 * wide]
        at = 8 * wide + 2 * hidden * layer
        up[layer] = grads[:, at : at + hidden]
        down[layer] = grads[:, at + hidden : at + 2 * hidden]


def end_kernel(attns, *refs):
    *parts, near, far = refs
    at = 0
    for part in parts[:attns]:
        wide = part.shape[1] // 2
        near[:, at : at + wide] = part[:, :wide]
        far[:, at : at + wide] = part[:, wide:]
        at += wide
    for part in parts[attns:]:
        near[:, at : at + part.shape[1]] = part[...]
        at += part.shape[1]


def end_sum_kernel(scal, near, by_zl, by_zh, by_both, mine, theirs):
    rows = mine.shape[0]
    wide = by_zh.shape[1]
    for core, out in ((scal[2], mine), (1 - scal[2], theirs)):
        cut = pl.ds(pl.multiple_of(core * rows, rows), rows)
        total = near[cut, :].astype(F32) + by_zl[cut, :].astype(F32)
        attn = total[:, :wide] + (by_zh[cut, :].astype(F32) + by_both[cut, :].astype(F32))
        out[:, :wide] = attn.astype(out.dtype)
        out[:, wide:] = total[:, wide:].astype(out.dtype)


def reduced_end(attns, feeds, scal, deps=(), later=()):
    rows, wide = attns[0].shape[0], sum(a.shape[1] // 2 for a in attns)
    whole = wide + sum(f.shape[1] for f in feeds)
    near, far = call(
        functools.partial(end_kernel, len(attns)),
        [shape((rows, whole), BF), shape((rows, wide), BF)],
        [VMEM] * (len(attns) + len(feeds)),
        [*attns, *feeds],
        deps=deps,
    )
    mine, theirs = call(
        end_sum_kernel,
        [shape((rows // 2, whole), F32), shape((rows // 2, whole), BF)],
        [SMEM] + [VMEM] * 4,
        [
            scal,
            near,
            sent_by(near, ZL, zl_is_not_core),
            sent_by(far, ZH, zl_is_core),
            sent_by(far, Z_MASK, zl_is_not_core),
        ],
        deps=later,
    )
    return mine, sent_by(theirs, CORE, zl_is_core)


def solution(mesh):
    in_specs = (
        P(("dp", "tensor"), None),
        P("dp"),
        P(None, "dp", None, "tensor"),
        P(None, "tensor", "dp"),
        P(None, "dp", "tensor"),
        P(None, "tensor", "dp"),
        P(None, None, ("dp", "tensor")),
        P(None, None, ("dp", "tensor")),
        P(("dp", "tensor"), None),
    )
    out_specs = (
        P(("dp", "tensor"), None),
        P(("dp", "tensor"), None),
        P(None, "dp", None, "tensor"),
        P(None, "tensor", "dp"),
        P(None, "dp", "tensor"),
        P(None, "tensor", "dp"),
        P(None, None, ("dp", "tensor")),
        P(None, None, ("dp", "tensor")),
    )
    return jax.shard_map(
        per_device, mesh=mesh, in_specs=in_specs, out_specs=out_specs, check_vma=False
    )
```
